32 devices in a mesh: freq: 8 (over z, y), sta: 4 (over x, core).
Axes of the slice: x: 2, y: 2, z: 4, core: 2. Of those that a mesh axis runs over, the one named last changes fastest.
Arguments:
- spectra: float32 [2, 128, 64, 8192], P(None, 'freq', None, 'sta'), may hold values from -24 to 24
- current: float32 [64, 2, 128, 512], P('freq', None, None, 'sta'), may hold values from -600 to 600, as said below
- previous: float32 [64, 2, 128, 512], P('freq', None, None, 'sta'), may hold values from -600 to 600, as said below
- table: int32 [64, 512], replicated, may hold values from 0 to 16383
- station_block: int32 [8192], P('sta'), may hold values from 0 to 63
- offsets: float32 [2, 8192], P(None, 'sta'), may hold values from -4 to 4
- slowness: float32 [2, 512], replicated, may hold values from -3 to 3
- weights: float32 [512], P('sta'), may hold values from 400 to 5000
- momentum: float32 [1], replicated, may hold values from 2 to 10
Outputs:
- estimate: float32 [64, 2, 128, 512], P('freq', None, None, 'sta')
- extrapolated: float32 [64, 2, 128, 512], P('freq', None, None, 'sta')
The draws below stay inside these ranges and needn't reach their ends.
Inputs may be any that keep to these rules, and one draw needn't show every extreme that they name: `current`: real values. `previous`: real values.
All inputs are finite; a program needn't handle non-finite values.
Results may differ from the reference program's by a relative error of at most 0.00105.
The reference program's roundings to bfloat16 on the way count: a program that leaves them out, or rounds other values in their place, can miss the bound.
Values may be sent and summed in bfloat16 or wider, within the bound.
A program may use at most 192 MiB of HBM per device.

```python
import math
import jax
import jax.numpy as jnp
from jax import lax

F = 64
CELLS = 512
W = 128
NB = 64
TMAX = 16384
STATIONS = 8192


def iterate_draw(key, stream_tag):
    shared = jax.random.fold_in(key, 101)
    bin_key, cell_key = jax.random.split(shared, 2)
    noise_key = jax.random.fold_in(key, stream_tag)
    bin_pos = jnp.arange(F, dtype=jnp.float32) / (F - 1)
    bin_scale = 10.0 ** bin_pos * jnp.exp(jax.random.uniform(bin_key, (F,), jnp.float32, -0.35, 0.35))
    cell_scale = 10.0 ** jax.random.uniform(cell_key, (CELLS,), jnp.float32)
    fluctuation = jnp.clip(jax.random.normal(noise_key, (F, 2, W, CELLS), jnp.float32), -4.0, 4.0)
    return fluctuation * bin_scale[:, None, None, None] * cell_scale[None, None, None, :]


def draw_current(key, part):
    return iterate_draw(key, 7)


def draw_previous(key, part):
    return iterate_draw(key, 13)


def plant(drawn, rng, low, top_value):
    longest = drawn.shape.index(max(drawn.shape))
    spots = []
    for shift in (0, 1):
        where = [jax.random.randint(jax.random.fold_in(rng, axis), (), 0, length) for axis, length in enumerate(drawn.shape)]
        where[longest] = (where[longest] + shift) % drawn.shape[longest]
        spots.append(tuple(where))
    return drawn.at[spots[0]].set(low).at[spots[1]].set(top_value)


def shard_levels(own_key, dims, cuts, smallest, top_value):
    level = 1.0
    for dim, blocks in cuts:
        heights = jax.random.uniform(jax.random.fold_in(jax.random.fold_in(own_key, 6), dim), (blocks,), jnp.float32, smallest / len(cuts), top_value / len(cuts))
        level = level * jnp.repeat(jnp.exp(heights), dims[dim] // blocks).reshape((-1,) + (1,) * (len(dims) - 1 - dim))
    return level


def noise(stream_key, dims, spread, reach, shards=(), kind=jnp.bfloat16):
    drawn = spread * jax.random.normal(stream_key, dims, jnp.float32)
    if shards:
        drawn = drawn * shard_levels(stream_key, dims, shards, -0.22, 0.18)
    return jnp.clip(drawn, -reach, reach).astype(kind)


def setup_inputs(seed: int = 0) -> dict:
    splits = jax.random.split(jax.random.key(seed), 10)
    spectra = noise(splits[0], (2, W, F, STATIONS), 4.0, 24.0, ((1, 8), (3, 4)), jnp.float32)
    current = draw_current(jax.random.fold_in(splits[9], 71), 0)
    previous = draw_previous(jax.random.fold_in(splits[9], 71), 0)
    table = plant(jax.random.randint(splits[3], (NB, CELLS), 0, TMAX), jax.random.fold_in(splits[3], 1), 0, TMAX - 1).astype(jnp.int32)
    station_block = plant(jax.random.randint(splits[4], (STATIONS,), 0, NB), jax.random.fold_in(splits[4], 1), 0, NB - 1).astype(jnp.int32)
    offsets = noise(splits[5], (2, STATIONS), 1.0, 4.0, ((1, 4),), jnp.float32)
    slowness = jnp.clip(jax.random.uniform(splits[6], (2, CELLS), jnp.float32, -3.0, 3.0), -3.0, 3.0)
    weights = jnp.clip(jnp.exp(math.log(5000.0) - 2.5257286 * jax.random.uniform(splits[7], (CELLS,), jnp.float32) ** shard_levels(splits[7], (CELLS,), ((0, 4),), -0.2, 0.2)), 400.0, 5000.0)
    momentum = jnp.clip(jax.random.uniform(splits[8], (1,), jnp.float32, 2.0, 10.0), 2.0, 10.0)
    return {"spectra": spectra, "current": current, "previous": previous, "table": table, "station_block": station_block, "offsets": offsets, "slowness": slowness, "weights": weights, "momentum": momentum}


def cell_block(cell_count):
    block_len = cell_count
    while block_len > 512 and block_len % 2 == 0:
        block_len = block_len // 2
    return block_len

def phases(number, delay_rows, off_rows, slow_cols, period):
    wrapped = number * delay_rows % period
    geometry = off_rows[0][:, None] * slow_cols[0][None, :] + off_rows[1][:, None] * slow_cols[1][None, :]
    phase_angle = (wrapped.astype(jnp.float32) + number.astype(jnp.float32) * geometry) * (2.0 * math.pi / period)
    return (jnp.cos(phase_angle).astype(jnp.bfloat16), jnp.sin(phase_angle).astype(jnp.bfloat16))

def forward_terms(cos_part, sin_part, iterate):
    window_count = iterate.shape[1]
    stacked = iterate.reshape(2 * window_count, iterate.shape[2])
    contract = (((1,), (1,)), ((), ()))
    with_cos = lax.dot_general(stacked, cos_part, contract, preferred_element_type=jnp.float32)
    with_sin = lax.dot_general(stacked, sin_part, contract, preferred_element_type=jnp.float32)
    real_part = with_cos[:window_count] + with_sin[window_count:]
    imag_part = with_cos[window_count:] - with_sin[:window_count]
    return jnp.stack([real_part, imag_part])

def adjoint_terms(cos_part, sin_part, residual):
    window_count = residual.shape[1]
    stacked = residual.reshape(2 * window_count, residual.shape[2])
    with_cos = jnp.dot(stacked, cos_part, preferred_element_type=jnp.float32)
    with_sin = jnp.dot(stacked, sin_part, preferred_element_type=jnp.float32)
    real_part = with_cos[:window_count] - with_sin[window_count:]
    imag_part = with_cos[window_count:] + with_sin[:window_count]
    return jnp.stack([real_part, imag_part])

def reference(spectra, current, previous, table, station_block, offsets, slowness, weights, momentum):
    period = 4 * F
    normalizer = 1.0 / math.sqrt(CELLS)
    block_len = cell_block(CELLS)
    relaid = jnp.transpose(spectra, (2, 0, 1, 3))

    def one_bin(bin_inputs):
        number, iterate, observed = bin_inputs
        iterate_b = iterate.astype(jnp.bfloat16)
        running = jnp.zeros((2, W, STATIONS), jnp.float32)
        for first_cell in range(0, CELLS, block_len):
            delay_rows = jnp.take(table[:, first_cell:first_cell + block_len], station_block, axis=0)
            cos_part, sin_part = phases(number, delay_rows, offsets, slowness[:, first_cell:first_cell + block_len], period)
            running = running + forward_terms(cos_part, sin_part, iterate_b[:, :, first_cell:first_cell + block_len])
        residual = (running * normalizer - observed).astype(jnp.bfloat16)
        pieces = []
        for first_cell in range(0, CELLS, block_len):
            delay_rows = jnp.take(table[:, first_cell:first_cell + block_len], station_block, axis=0)
            cos_part, sin_part = phases(number, delay_rows, offsets, slowness[:, first_cell:first_cell + block_len], period)
            pieces.append(adjoint_terms(cos_part, sin_part, residual) * normalizer)
        return jnp.concatenate(pieces, axis=2)
    numbers = jnp.arange(1, F + 1, dtype=jnp.int32)
    gradient = lax.map(one_bin, (numbers, current, relaid))
    step_size = CELLS / (math.sqrt(STATIONS) + math.sqrt(CELLS)) ** 2
    stepped = current - step_size * gradient
    group_norm = jnp.sqrt(lax.optimization_barrier(jnp.sum(stepped * stepped, axis=(0, 1))) + 1e-06)
    estimate = stepped * jnp.maximum(0.0, 1.0 - step_size * weights[None, :] / group_norm)
    momentum_now = momentum[0]
    momentum_next = (1.0 + jnp.sqrt(1.0 + 4.0 * momentum_now * momentum_now)) / 2.0
    extrapolated = estimate + (momentum_now - 1.0) / momentum_next * (estimate - previous)
    return (estimate, extrapolated)
```

```python
import functools
import math

import jax
import jax.numpy as jnp
from jax import lax
from jax.experimental import pallas as pl
from jax.experimental.pallas import tpu as pltpu
from jax.sharding import PartitionSpec as P

F = 64
CELLS = 512


def cell_block(cell_count):
    block_len = cell_count
    while block_len > 512 and block_len % 2 == 0:
        block_len = block_len // 2
    return block_len


def phases(number, delay_rows, off_rows, slow_cols, period):
    wrapped = number * delay_rows % period
    geometry = (
        off_rows[0][:, None] * slow_cols[0][None, :] + off_rows[1][:, None] * slow_cols[1][None, :]
    )
    phase_angle = (wrapped.astype(jnp.float32) + number.astype(jnp.float32) * geometry) * (
        2.0 * math.pi / period
    )
    return (jnp.cos(phase_angle).astype(jnp.bfloat16), jnp.sin(phase_angle).astype(jnp.bfloat16))


def forward_terms(cos_part, sin_part, iterate):
    window_count = iterate.shape[1]
    stacked = iterate.reshape(2 * window_count, iterate.shape[2])
    contract = (((1,), (1,)), ((), ()))
    with_cos = lax.dot_general(stacked, cos_part, contract, preferred_element_type=jnp.float32)
    with_sin = lax.dot_general(stacked, sin_part, contract, preferred_element_type=jnp.float32)
    real_part = with_cos[:window_count] + with_sin[window_count:]
    imag_part = with_cos[window_count:] - with_sin[:window_count]
    return jnp.stack([real_part, imag_part])


def adjoint_terms(cos_part, sin_part, residual):
    window_count = residual.shape[1]
    stacked = residual.reshape(2 * window_count, residual.shape[2])
    with_cos = jnp.dot(stacked, cos_part, preferred_element_type=jnp.float32)
    with_sin = jnp.dot(stacked, sin_part, preferred_element_type=jnp.float32)
    real_part = with_cos[:window_count] - with_sin[window_count:]
    imag_part = with_cos[window_count:] + with_sin[:window_count]
    return jnp.stack([real_part, imag_part])


def local(spectra, current, previous, table, station_block, offsets, slowness, weights, momentum):
    period = 4 * F
    normalizer = 1.0 / math.sqrt(CELLS)
    bin_count = current.shape[0]
    cell_share = current.shape[3]
    stations_here = station_block.shape[0]
    station_total = stations_here * lax.axis_size("sta")
    first_bin = lax.axis_index("freq") * bin_count
    relaid = lax.all_to_all(
        spectra.astype(jnp.bfloat16), "freq", split_axis=2, concat_axis=1, tiled=True
    ).astype(spectra.dtype)
    iterate_b = current.astype(jnp.bfloat16)
    segment = lax.all_gather(iterate_b, "sta", axis=3, tiled=True)
    cell_count = segment.shape[3]
    block_len = cell_block(cell_count)
    delay_rows = jnp.take(table, station_block, axis=0)
    bin_terms = []
    cos_blocks = []
    sin_blocks = []
    for add_bin_index in range(bin_count):
        cos_part, sin_part = phases(
            first_bin + add_bin_index + 1, delay_rows, offsets, slowness, period
        )
        cos_blocks.append(cos_part)
        sin_blocks.append(sin_part)
        bin_terms.append(
            forward_terms(cos_part, sin_part, segment[add_bin_index, :, :, 0:block_len])
        )
    running = jnp.stack(bin_terms)
    cos_all = jnp.stack(cos_blocks)
    sin_all = jnp.stack(sin_blocks)
    predicted, cos_all, sin_all = (running, cos_all, sin_all)
    bin_sums = []
    for bin_index in range(bin_count):
        residual = (predicted[bin_index] * normalizer - relaid[:, :, bin_index, :]).astype(
            jnp.bfloat16
        )
        bin_sums.append(
            adjoint_terms(cos_all[bin_index], sin_all[bin_index], residual) * normalizer
        )
    partial_sums = jnp.stack(bin_sums)
    summed = lax.psum(partial_sums, "sta")
    gradient = lax.dynamic_slice_in_dim(summed, lax.axis_index("sta") * cell_share, cell_share, 3)
    step_size = CELLS / (math.sqrt(station_total) + math.sqrt(CELLS)) ** 2
    stepped = current - step_size * gradient
    threshold = step_size * weights
    squares = jnp.sum(stepped * stepped, axis=(0, 1))
    group_norm = jnp.sqrt(lax.psum(squares, "freq") + 1e-06)
    estimate = stepped * jnp.maximum(0.0, 1.0 - threshold[None, :] / group_norm)
    momentum_now = momentum[0]
    momentum_next = (1.0 + jnp.sqrt(1.0 + 4.0 * momentum_now * momentum_now)) / 2.0
    extrapolated = estimate + (momentum_now - 1.0) / momentum_next * (estimate - previous)
    return (estimate, extrapolated)


SIN_TERMS = (3.1415926535362892, -5.167712764624382, 2.5501633189428987, -0.5992521977810126, 0.08205040162239277, -0.007028386120383206)
COS_TERMS = (0.9999999997799041, -4.934802137078749, 4.058709159554242, -1.335212003029471, 0.23493731372678894, -0.024396324214549327)


def horner(terms, u):
    total = jnp.full_like(u, terms[-1])
    for term in terms[-2::-1]:
        total = total * u + term
    return total


def turns_cos_sin(turns):
    part = turns - jnp.round(turns)
    square = part * part
    half_sin = part * horner(SIN_TERMS, square)
    half_cos = horner(COS_TERMS, square)
    doubled = half_sin + half_sin
    return 1.0 - doubled * half_sin, doubled * half_cos


def bins_kernel(
    period, normalizer, place_ref, blocks_ref, off_ref, tab_ref, slow_ref, x_ref, o0, o1, o2, o3, g_ref,
    delay_ref, cos_ref, sin_ref, pred_ref, res_ref
):
    bins, cells, tile = cos_ref.shape
    number = place_ref[0].astype(jnp.float32)
    spot = place_ref[1]
    windows = x_ref.shape[1] // 2
    piece = o0.shape[2]
    step = pl.program_id(0)

    @pl.when(step == 0)
    def _():
        g_ref[...] = jnp.zeros_like(g_ref)

    rows = lax.broadcasted_iota(jnp.int32, (tab_ref.shape[1], tile), 0)
    picks = jnp.where(rows == blocks_ref[...], 1.0, 0.0).astype(jnp.bfloat16)
    delay_ref[...] = jnp.dot(tab_ref[...], picks, preferred_element_type=jnp.float32)
    scale = 1.0 / period
    strip = 16
    lanes = 256

    def fill(index, _):
        row = pl.ds(pl.multiple_of(index // (tile // lanes) * strip, strip), strip)
        col = pl.ds(pl.multiple_of(index % (tile // lanes) * lanes, lanes), lanes)
        slow = slow_ref[row, :]
        geometry = off_ref[0:1, col] * slow[:, 0:1] + off_ref[1:2, col] * slow[:, 1:2]
        delay = delay_ref[row, col]
        unit_cos, unit_sin = turns_cos_sin((delay + geometry) * scale)
        turns = number * delay * scale
        turns = (turns - jnp.round(turns)) + number * geometry * scale
        cos_old, sin_old = turns_cos_sin(turns)
        cos_ref[0, row, col] = cos_old.astype(jnp.bfloat16)
        sin_ref[0, row, col] = sin_old.astype(jnp.bfloat16)
        cos_now = cos_old * unit_cos - sin_old * unit_sin
        sin_now = sin_old * unit_cos + cos_old * unit_sin
        twice = unit_cos + unit_cos
        for b in range(1, bins):
            cos_ref[b, row, col] = cos_now.astype(jnp.bfloat16)
            sin_ref[b, row, col] = sin_now.astype(jnp.bfloat16)
            if b < bins - 1:
                cos_now, cos_old = twice * cos_now - cos_old, cos_now
                sin_now, sin_old = twice * sin_now - sin_old, sin_now
        return 0

    lax.fori_loop(0, cells // strip * (tile // lanes), fill, 0)

    across = (((1,), (1,)), ((), ()))

    for b in range(bins):
        stacked = x_ref[b]
        with_cos = jnp.dot(stacked, cos_ref[b], preferred_element_type=jnp.float32)
        with_sin = jnp.dot(stacked, sin_ref[b], preferred_element_type=jnp.float32)
        pred_ref[b, 0:windows] = (with_cos[:windows] + with_sin[windows:]) * normalizer
        pred_ref[b, windows:] = (with_cos[windows:] - with_sin[:windows]) * normalizer
        for d, o_ref in enumerate((o0, o1, o2, o3)):
            first = jnp.bitwise_xor(spot, d) * piece
            for k in range(2):
                at = pl.ds(pl.multiple_of(first + k * windows, piece), piece)
                res_ref[b, at, :] = (pred_ref[b, at, :] - o_ref[b, k].astype(jnp.float32)).astype(jnp.bfloat16)
        residual = res_ref[b]
        back_cos = lax.dot_general(residual, cos_ref[b], across, preferred_element_type=jnp.float32)
        back_sin = lax.dot_general(residual, sin_ref[b], across, preferred_element_type=jnp.float32)
        g_ref[b, 0:windows] += back_cos[:windows] - back_sin[windows:]
        g_ref[b, windows:] += back_cos[windows:] + back_sin[:windows]


def bins_gradient(place, blocks, offsets, tab, slow, iterate, observed, period, normalizer):
    bins, rows, cells = iterate.shape
    stations = blocks.shape[1]
    piece = observed[0].shape[2]
    tile = 512
    vm = pltpu.VMEM
    whole = lambda shape: pl.BlockSpec(shape, lambda i: (0,) * len(shape))
    return pl.pallas_call(
        functools.partial(bins_kernel, period, normalizer),
        grid=(stations // tile,),
        out_shape=jax.ShapeDtypeStruct((bins, rows, cells), jnp.float32),
        in_specs=[
            pl.BlockSpec(memory_space=pltpu.SMEM),
            pl.BlockSpec((1, tile), lambda i: (0, i)),
            pl.BlockSpec((2, tile), lambda i: (0, i)),
            whole(tab.shape),
            whole(slow.shape),
            whole(iterate.shape),
        ]
        + [pl.BlockSpec((bins, 2, piece, tile), lambda i: (0, 0, 0, i))] * 4,
        out_specs=whole((bins, rows, cells)),
        scratch_shapes=[
            vm((cells, tile), jnp.float32),
            vm((bins, cells, tile), jnp.bfloat16),
            vm((bins, cells, tile), jnp.bfloat16),
            vm((bins, rows, tile), jnp.float32),
            vm((bins, rows, tile), jnp.bfloat16),
        ],
        compiler_params=pltpu.CompilerParams(vmem_limit_bytes=52 * 2**20),
        cost_estimate=pl.CostEstimate(
            flops=8 * bins * rows * cells * stations, bytes_accessed=16 * 2**20, transcendentals=0
        ),
    )(place, blocks, offsets, tab, slow, iterate, *observed)


def local_grouped(freq_size, sta_size, spectra, current, previous, table, station_block, offsets, slowness, weights, momentum):
    period = 4 * F
    normalizer = 1.0 / math.sqrt(CELLS)
    bins = current.shape[0]
    cell_share = current.shape[3]
    half_windows = current.shape[2] // 2
    stations_here = station_block.shape[0]
    station_total = stations_here * sta_size
    me = lax.axis_index("freq")
    mine = lax.axis_index("sta")
    half, spot = me // 4, me % 4
    gradient_back = []
    rounded = current.astype(jnp.bfloat16)
    tab = jnp.bitwise_and(table, period - 1).astype(jnp.bfloat16).T
    slow = slowness.T
    blocks = station_block.reshape(1, -1)
    picks = []
    iterates = []
    for c in range(2):
        give = lax.rem(me + c, 2)
        sent = lax.dynamic_slice_in_dim(rounded, give * half_windows, half_windows, 2)
        perm = [(f, ((f + c) % 2) * 4 + f // 2) for f in range(freq_size)]
        got = lax.ppermute(sent, "freq", perm)
        iterates.append(lax.all_gather(got, "sta", axis=3, tiled=True))
        gradient_back.append([(b, a) for a, b in perm])
    observed = []
    for c in range(2):
        odd = lax.rem(half + c, 2)
        parts = []
        for d in range(4):
            first = (2 * jnp.bitwise_xor(spot, d) + odd) * bins
            part = lax.dynamic_slice_in_dim(spectra, first, bins, 2).astype(jnp.bfloat16)
            part = jnp.transpose(part, (2, 0, 1, 3))
            if d:
                part = lax.ppermute(part, "freq", [(f, f ^ d) for f in range(freq_size)])
            parts.append(part)
        observed.append(parts)
    halves = []
    for c in range(2):
        odd = lax.rem(half + c, 2)
        place = jnp.stack([(2 * spot + odd) * bins + 1, spot]).astype(jnp.int32)
        iterate = iterates[c].reshape(bins, 2 * half_windows, cell_share * sta_size)
        partial = bins_gradient(
            place, blocks, offsets, tab, slow, iterate, observed[c], period, normalizer
        )
        total = lax.dynamic_slice_in_dim(partial, mine * cell_share, cell_share, 2)
        for d in range(1, sta_size):
            sent = lax.dynamic_slice_in_dim(
                partial, jnp.bitwise_xor(mine, d) * cell_share, cell_share, 2
            )
            total = total + lax.ppermute(sent, "sta", [(s, s ^ d) for s in range(sta_size)])
        home = lax.ppermute(total * normalizer, "freq", gradient_back[c])
        halves.append(home.reshape(bins, 2, half_windows, cell_share))
    even = lax.rem(me, 2) == 0
    gradient = jnp.concatenate(
        [jnp.where(even, halves[0], halves[1]), jnp.where(even, halves[1], halves[0])], axis=2
    )
    step_size = CELLS / (math.sqrt(station_total) + math.sqrt(CELLS)) ** 2
    stepped = current - step_size * gradient
    threshold = step_size * weights
    squares = jnp.sum(stepped * stepped, axis=(0, 1))
    for d in (1, 2, 4):
        squares = squares + lax.ppermute(squares, "freq", [(f, f ^ d) for f in range(freq_size)])
    group_norm = jnp.sqrt(squares + 1e-06)
    estimate = stepped * jnp.maximum(0.0, 1.0 - threshold[None, :] / group_norm)
    momentum_now = momentum[0]
    momentum_next = (1.0 + jnp.sqrt(1.0 + 4.0 * momentum_now * momentum_now)) / 2.0
    extrapolated = estimate + (momentum_now - 1.0) / momentum_next * (estimate - previous)
    return (estimate, extrapolated)


def solution(mesh):
    freq_size, sta_size = mesh.shape["freq"], mesh.shape["sta"]
    body = local
    if freq_size == 8 and sta_size == 4:
        body = functools.partial(local_grouped, freq_size, sta_size)
    in_specs = (
        P(None, "freq", None, "sta"),
        P("freq", None, None, "sta"),
        P("freq", None, None, "sta"),
        P(),
        P("sta"),
        P(None, "sta"),
        P(),
        P("sta"),
        P(),
    )
    out_specs = (P("freq", None, None, "sta"), P("freq", None, None, "sta"))
    return jax.shard_map(body, mesh=mesh, in_specs=in_specs, out_specs=out_specs, check_vma=False)
```

```python
import functools
import math

import jax
import jax.numpy as jnp
from jax import lax
from jax.experimental import pallas as pl
from jax.experimental.pallas import tpu as pltpu
from jax.sharding import PartitionSpec as P

F = 64
CELLS = 512


def cell_block(cell_count):
    block_len = cell_count
    while block_len > 512 and block_len % 2 == 0:
        block_len = block_len // 2
    return block_len


def phases(number, delay_rows, off_rows, slow_cols, period):
    wrapped = number * delay_rows % period
    geometry = (
        off_rows[0][:, None] * slow_cols[0][None, :] + off_rows[1][:, None] * slow_cols[1][None, :]
    )
    phase_angle = (wrapped.astype(jnp.float32) + number.astype(jnp.float32) * geometry) * (
        2.0 * math.pi / period
    )
    return (jnp.cos(phase_angle).astype(jnp.bfloat16), jnp.sin(phase_angle).astype(jnp.bfloat16))


def forward_terms(cos_part, sin_part, iterate):
    window_count = iterate.shape[1]
    stacked = iterate.reshape(2 * window_count, iterate.shape[2])
    contract = (((1,), (1,)), ((), ()))
    with_cos = lax.dot_general(stacked, cos_part, contract, preferred_element_type=jnp.float32)
    with_sin = lax.dot_general(stacked, sin_part, contract, preferred_element_type=jnp.float32)
    real_part = with_cos[:window_count] + with_sin[window_count:]
    imag_part = with_cos[window_count:] - with_sin[:window_count]
    return jnp.stack([real_part, imag_part])


def adjoint_terms(cos_part, sin_part, residual):
    window_count = residual.shape[1]
    stacked = residual.reshape(2 * window_count, residual.shape[2])
    with_cos = jnp.dot(stacked, cos_part, preferred_element_type=jnp.float32)
    with_sin = jnp.dot(stacked, sin_part, preferred_element_type=jnp.float32)
    real_part = with_cos[:window_count] - with_sin[window_count:]
    imag_part = with_cos[window_count:] + with_sin[:window_count]
    return jnp.stack([real_part, imag_part])


def local(spectra, current, previous, table, station_block, offsets, slowness, weights, momentum):
    period = 4 * F
    normalizer = 1.0 / math.sqrt(CELLS)
    bin_count = current.shape[0]
    cell_share = current.shape[3]
    stations_here = station_block.shape[0]
    station_total = stations_here * lax.axis_size("sta")
    first_bin = lax.axis_index("freq") * bin_count
    relaid = lax.all_to_all(
        spectra.astype(jnp.bfloat16), "freq", split_axis=2, concat_axis=1, tiled=True
    ).astype(spectra.dtype)
    iterate_b = current.astype(jnp.bfloat16)
    segment = lax.all_gather(iterate_b, "sta", axis=3, tiled=True)
    cell_count = segment.shape[3]
    block_len = cell_block(cell_count)
    delay_rows = jnp.take(table, station_block, axis=0)
    bin_terms = []
    cos_blocks = []
    sin_blocks = []
    for add_bin_index in range(bin_count):
        cos_part, sin_part = phases(
            first_bin + add_bin_index + 1, delay_rows, offsets, slowness, period
        )
        cos_blocks.append(cos_part)
        sin_blocks.append(sin_part)
        bin_terms.append(
            forward_terms(cos_part, sin_part, segment[add_bin_index, :, :, 0:block_len])
        )
    running = jnp.stack(bin_terms)
    cos_all = jnp.stack(cos_blocks)
    sin_all = jnp.stack(sin_blocks)
    predicted, cos_all, sin_all = (running, cos_all, sin_all)
    bin_sums = []
    for bin_index in range(bin_count):
        residual = (predicted[bin_index] * normalizer - relaid[:, :, bin_index, :]).astype(
            jnp.bfloat16
        )
        bin_sums.append(
            adjoint_terms(cos_all[bin_index], sin_all[bin_index], residual) * normalizer
        )
    partial_sums = jnp.stack(bin_sums)
    summed = lax.psum(partial_sums, "sta")
    gradient = lax.dynamic_slice_in_dim(summed, lax.axis_index("sta") * cell_share, cell_share, 3)
    step_size = CELLS / (math.sqrt(station_total) + math.sqrt(CELLS)) ** 2
    stepped = current - step_size * gradient
    threshold = step_size * weights
    squares = jnp.sum(stepped * stepped, axis=(0, 1))
    group_norm = jnp.sqrt(lax.psum(squares, "freq") + 1e-06)
    estimate = stepped * jnp.maximum(0.0, 1.0 - threshold[None, :] / group_norm)
    momentum_now = momentum[0]
    momentum_next = (1.0 + jnp.sqrt(1.0 + 4.0 * momentum_now * momentum_now)) / 2.0
    extrapolated = estimate + (momentum_now - 1.0) / momentum_next * (estimate - previous)
    return (estimate, extrapolated)


SIN_TERMS = (3.1415926535362892, -5.167712764624382, 2.5501633189428987, -0.5992521977810126, 0.08205040162239277, -0.007028386120383206)
COS_TERMS = (0.9999999997799041, -4.934802137078749, 4.058709159554242, -1.335212003029471, 0.23493731372678894, -0.024396324214549327)


def horner(terms, u):
    total = jnp.full_like(u, terms[-1])
    for term in terms[-2::-1]:
        total = total * u + term
    return total


def turns_cos_sin(turns):
    part = turns - jnp.round(turns)
    square = part * part
    half_sin = part * horner(SIN_TERMS, square)
    half_cos = horner(COS_TERMS, square)
    doubled = half_sin + half_sin
    return 1.0 - doubled * half_sin, doubled * half_cos


def bins_kernel(
    period, normalizer, place_ref, blocks_ref, off_ref, tab_ref, slow_ref, x_ref, o0, o1, o2, o3, g_ref,
    delay_ref, cos_ref, sin_ref, pred_ref, res_ref
):
    bins, cells, tile = cos_ref.shape
    number = place_ref[0].astype(jnp.float32)
    spot = place_ref[1]
    windows = x_ref.shape[1] // 2
    piece = o0.shape[2]
    step = pl.program_id(0)

    @pl.when(step == 0)
    def _():
        g_ref[...] = jnp.zeros_like(g_ref)

    rows = lax.broadcasted_iota(jnp.int32, (tab_ref.shape[1], tile), 0)
    picks = jnp.where(rows == blocks_ref[...], 1.0, 0.0).astype(jnp.bfloat16)
    delay_ref[...] = jnp.dot(tab_ref[...], picks, preferred_element_type=jnp.float32)
    scale = 1.0 / period
    strip = 16
    lanes = 256

    def fill(index, _):
        row = pl.ds(pl.multiple_of(index // (tile // lanes) * strip, strip), strip)
        col = pl.ds(pl.multiple_of(index % (tile // lanes) * lanes, lanes), lanes)
        slow = slow_ref[row, :]
        geometry = off_ref[0:1, col] * slow[:, 0:1] + off_ref[1:2, col] * slow[:, 1:2]
        delay = delay_ref[row, col]
        unit_cos, unit_sin = turns_cos_sin((delay + geometry) * scale)
        turns = number * delay * scale
        turns = (turns - jnp.round(turns)) + number * geometry * scale
        cos_old, sin_old = turns_cos_sin(turns)
        cos_ref[0, row, col] = cos_old.astype(jnp.bfloat16)
        sin_ref[0, row, col] = sin_old.astype(jnp.bfloat16)
        cos_now = cos_old * unit_cos - sin_old * unit_sin
        sin_now = sin_old * unit_cos + cos_old * unit_sin
        twice = unit_cos + unit_cos
        for b in range(1, bins):
            cos_ref[b, row, col] = cos_now.astype(jnp.bfloat16)
            sin_ref[b, row, col] = sin_now.astype(jnp.bfloat16)
            if b < bins - 1:
                cos_now, cos_old = twice * cos_now - cos_old, cos_now
                sin_now, sin_old = twice * sin_now - sin_old, sin_now
        return 0

    lax.fori_loop(0, cells // strip * (tile // lanes), fill, 0, unroll=2)

    across = (((1,), (1,)), ((), ()))

    for b in range(bins):
        stacked = x_ref[b]
        with_cos = jnp.dot(stacked, cos_ref[b], preferred_element_type=jnp.float32)
        with_sin = jnp.dot(stacked, sin_ref[b], preferred_element_type=jnp.float32)
        pred_ref[b, 0:windows] = (with_cos[:windows] + with_sin[windows:]) * normalizer
        pred_ref[b, windows:] = (with_cos[windows:] - with_sin[:windows]) * normalizer
        for d, o_ref in enumerate((o0, o1, o2, o3)):
            first = jnp.bitwise_xor(spot, d) * piece
            for k in range(2):
                at = pl.ds(pl.multiple_of(first + k * windows, piece), piece)
                res_ref[b, at, :] = (pred_ref[b, at, :] - o_ref[b, k].astype(jnp.float32)).astype(jnp.bfloat16)
        residual = res_ref[b]
        back_cos = lax.dot_general(residual, cos_ref[b], across, preferred_element_type=jnp.float32)
        back_sin = lax.dot_general(residual, sin_ref[b], across, preferred_element_type=jnp.float32)
        g_ref[b, 0:windows] += back_cos[:windows] - back_sin[windows:]
        g_ref[b, windows:] += back_cos[windows:] + back_sin[:windows]


def bins_gradient(place, blocks, offsets, tab, slow, iterate, observed, period, normalizer):
    bins, rows, cells = iterate.shape
    stations = blocks.shape[1]
    piece = observed[0].shape[2]
    tile = 512
    vm = pltpu.VMEM
    whole = lambda shape: pl.BlockSpec(shape, lambda i: (0,) * len(shape))
    return pl.pallas_call(
        functools.partial(bins_kernel, period, normalizer),
        grid=(stations // tile,),
        out_shape=jax.ShapeDtypeStruct((bins, rows, cells), jnp.float32),
        in_specs=[
            pl.BlockSpec(memory_space=pltpu.SMEM),
            pl.BlockSpec((1, tile), lambda i: (0, i)),
            pl.BlockSpec((2, tile), lambda i: (0, i)),
            whole(tab.shape),
            whole(slow.shape),
            whole(iterate.shape),
        ]
        + [pl.BlockSpec((bins, 2, piece, tile), lambda i: (0, 0, 0, i))] * 4,
        out_specs=whole((bins, rows, cells)),
        scratch_shapes=[
            vm((cells, tile), jnp.float32),
            vm((bins, cells, tile), jnp.bfloat16),
            vm((bins, cells, tile), jnp.bfloat16),
            vm((bins, rows, tile), jnp.float32),
            vm((bins, rows, tile), jnp.bfloat16),
        ],
        compiler_params=pltpu.CompilerParams(vmem_limit_bytes=52 * 2**20),
        cost_estimate=pl.CostEstimate(
            flops=8 * bins * rows * cells * stations, bytes_accessed=16 * 2**20, transcendentals=0
        ),
    )(place, blocks, offsets, tab, slow, iterate, *observed)


def local_grouped(freq_size, sta_size, spectra, current, previous, table, station_block, offsets, slowness, weights, momentum):
    period = 4 * F
    normalizer = 1.0 / math.sqrt(CELLS)
    bins = current.shape[0]
    cell_share = current.shape[3]
    half_windows = current.shape[2] // 2
    stations_here = station_block.shape[0]
    station_total = stations_here * sta_size
    me = lax.axis_index("freq")
    mine = lax.axis_index("sta")
    half, spot = me // 4, me % 4
    gradient_back = []
    rounded = current.astype(jnp.bfloat16)
    tab = jnp.bitwise_and(table, period - 1).astype(jnp.bfloat16).T
    slow = slowness.T
    blocks = station_block.reshape(1, -1)
    picks = []
    iterates = []
    for c in range(2):
        give = lax.rem(me + c, 2)
        sent = lax.dynamic_slice_in_dim(rounded, give * half_windows, half_windows, 2)
        perm = [(f, ((f + c) % 2) * 4 + f // 2) for f in range(freq_size)]
        got = lax.ppermute(sent, "freq", perm)
        iterates.append(got)
        gradient_back.append([(b, a) for a, b in perm])
    observed = []
    for c in range(2):
        odd = lax.rem(half + c, 2)
        parts = []
        for d in range(4):
            first = (2 * jnp.bitwise_xor(spot, d) + odd) * bins
            part = lax.dynamic_slice_in_dim(spectra, first, bins, 2).astype(jnp.bfloat16)
            parts.append(jnp.transpose(part, (2, 0, 1, 3)))
        if c == 0:
            parts, iterates = lax.optimization_barrier((parts, iterates))
            iterates = lax.all_gather(jnp.stack(iterates), "sta", axis=4, tiled=True)
        for d in range(1, 4):
            parts[d] = lax.ppermute(parts[d], "freq", [(f, f ^ d) for f in range(freq_size)])
        observed.append(parts)
    halves = []
    for c in range(2):
        odd = lax.rem(half + c, 2)
        place = jnp.stack([(2 * spot + odd) * bins + 1, spot]).astype(jnp.int32)
        iterate = iterates[c].reshape(bins, 2 * half_windows, cell_share * sta_size)
        partial = bins_gradient(
            place, blocks, offsets, tab, slow, iterate, observed[c], period, normalizer
        )
        total = lax.dynamic_slice_in_dim(partial, mine * cell_share, cell_share, 2)
        for d in range(1, sta_size):
            sent = lax.dynamic_slice_in_dim(
                partial, jnp.bitwise_xor(mine, d) * cell_share, cell_share, 2
            )
            total = total + lax.ppermute(sent, "sta", [(s, s ^ d) for s in range(sta_size)])
        home = lax.ppermute(total * normalizer, "freq", gradient_back[c])
        halves.append(home.reshape(bins, 2, half_windows, cell_share))
    even = lax.rem(me, 2) == 0
    gradient = jnp.concatenate(
        [jnp.where(even, halves[0], halves[1]), jnp.where(even, halves[1], halves[0])], axis=2
    )
    step_size = CELLS / (math.sqrt(station_total) + math.sqrt(CELLS)) ** 2
    stepped = current - step_size * gradient
    threshold = step_size * weights
    squares = jnp.sum(stepped * stepped, axis=(0, 1))
    for d in (1, 2, 4):
        squares = squares + lax.ppermute(squares, "freq", [(f, f ^ d) for f in range(freq_size)])
    group_norm = jnp.sqrt(squares + 1e-06)
    estimate = stepped * jnp.maximum(0.0, 1.0 - threshold[None, :] / group_norm)
    momentum_now = momentum[0]
    momentum_next = (1.0 + jnp.sqrt(1.0 + 4.0 * momentum_now * momentum_now)) / 2.0
    extrapolated = estimate + (momentum_now - 1.0) / momentum_next * (estimate - previous)
    return (estimate, extrapolated)


def solution(mesh):
    freq_size, sta_size = mesh.shape["freq"], mesh.shape["sta"]
    body = local
    if freq_size == 8 and sta_size == 4:
        body = functools.partial(local_grouped, freq_size, sta_size)
    in_specs = (
        P(None, "freq", None, "sta"),
        P("freq", None, None, "sta"),
        P("freq", None, None, "sta"),
        P(),
        P("sta"),
        P(None, "sta"),
        P(),
        P("sta"),
        P(),
    )
    out_specs = (P("freq", None, None, "sta"), P("freq", None, None, "sta"))
    return jax.shard_map(body, mesh=mesh, in_specs=in_specs, out_specs=out_specs, check_vma=False)
```

```python
import functools
import math

import jax
import jax.numpy as jnp
from jax import lax
from jax.experimental import pallas as pl
from jax.experimental.pallas import tpu as pltpu
from jax.sharding import PartitionSpec as P

F = 64
CELLS = 512


def cell_block(cell_count):
    block_len = cell_count
    while block_len > 512 and block_len % 2 == 0:
        block_len = block_len // 2
    return block_len


def phases(number, delay_rows, off_rows, slow_cols, period):
    wrapped = number * delay_rows % period
    geometry = (
        off_rows[0][:, None] * slow_cols[0][None, :] + off_rows[1][:, None] * slow_cols[1][None, :]
    )
    phase_angle = (wrapped.astype(jnp.float32) + number.astype(jnp.float32) * geometry) * (
        2.0 * math.pi / period
    )
    return (jnp.cos(phase_angle).astype(jnp.bfloat16), jnp.sin(phase_angle).astype(jnp.bfloat16))


def forward_terms(cos_part, sin_part, iterate):
    window_count = iterate.shape[1]
    stacked = iterate.reshape(2 * window_count, iterate.shape[2])
    contract = (((1,), (1,)), ((), ()))
    with_cos = lax.dot_general(stacked, cos_part, contract, preferred_element_type=jnp.float32)
    with_sin = lax.dot_general(stacked, sin_part, contract, preferred_element_type=jnp.float32)
    real_part = with_cos[:window_count] + with_sin[window_count:]
    imag_part = with_cos[window_count:] - with_sin[:window_count]
    return jnp.stack([real_part, imag_part])


def adjoint_terms(cos_part, sin_part, residual):
    window_count = residual.shape[1]
    stacked = residual.reshape(2 * window_count, residual.shape[2])
    with_cos = jnp.dot(stacked, cos_part, preferred_element_type=jnp.float32)
    with_sin = jnp.dot(stacked, sin_part, preferred_element_type=jnp.float32)
    real_part = with_cos[:window_count] - with_sin[window_count:]
    imag_part = with_cos[window_count:] + with_sin[:window_count]
    return jnp.stack([real_part, imag_part])


def local(spectra, current, previous, table, station_block, offsets, slowness, weights, momentum):
    period = 4 * F
    normalizer = 1.0 / math.sqrt(CELLS)
    bin_count = current.shape[0]
    cell_share = current.shape[3]
    stations_here = station_block.shape[0]
    station_total = stations_here * lax.axis_size("sta")
    first_bin = lax.axis_index("freq") * bin_count
    relaid = lax.all_to_all(
        spectra.astype(jnp.bfloat16), "freq", split_axis=2, concat_axis=1, tiled=True
    ).astype(spectra.dtype)
    iterate_b = current.astype(jnp.bfloat16)
    segment = lax.all_gather(iterate_b, "sta", axis=3, tiled=True)
    cell_count = segment.shape[3]
    block_len = cell_block(cell_count)
    delay_rows = jnp.take(table, station_block, axis=0)
    bin_terms = []
    cos_blocks = []
    sin_blocks = []
    for add_bin_index in range(bin_count):
        cos_part, sin_part = phases(
            first_bin + add_bin_index + 1, delay_rows, offsets, slowness, period
        )
        cos_blocks.append(cos_part)
        sin_blocks.append(sin_part)
        bin_terms.append(
            forward_terms(cos_part, sin_part, segment[add_bin_index, :, :, 0:block_len])
        )
    running = jnp.stack(bin_terms)
    cos_all = jnp.stack(cos_blocks)
    sin_all = jnp.stack(sin_blocks)
    predicted, cos_all, sin_all = (running, cos_all, sin_all)
    bin_sums = []
    for bin_index in range(bin_count):
        residual = (predicted[bin_index] * normalizer - relaid[:, :, bin_index, :]).astype(
            jnp.bfloat16
        )
        bin_sums.append(
            adjoint_terms(cos_all[bin_index], sin_all[bin_index], residual) * normalizer
        )
    partial_sums = jnp.stack(bin_sums)
    summed = lax.psum(partial_sums, "sta")
    gradient = lax.dynamic_slice_in_dim(summed, lax.axis_index("sta") * cell_share, cell_share, 3)
    step_size = CELLS / (math.sqrt(station_total) + math.sqrt(CELLS)) ** 2
    stepped = current - step_size * gradient
    threshold = step_size * weights
    squares = jnp.sum(stepped * stepped, axis=(0, 1))
    group_norm = jnp.sqrt(lax.psum(squares, "freq") + 1e-06)
    estimate = stepped * jnp.maximum(0.0, 1.0 - threshold[None, :] / group_norm)
    momentum_now = momentum[0]
    momentum_next = (1.0 + jnp.sqrt(1.0 + 4.0 * momentum_now * momentum_now)) / 2.0
    extrapolated = estimate + (momentum_now - 1.0) / momentum_next * (estimate - previous)
    return (estimate, extrapolated)


SIN_TERMS = (3.1415926535362892, -5.167712764624382, 2.5501633189428987, -0.5992521977810126, 0.08205040162239277, -0.007028386120383206)
COS_TERMS = (0.9999999997799041, -4.934802137078749, 4.058709159554242, -1.335212003029471, 0.23493731372678894, -0.024396324214549327)


def horner(terms, u):
    total = jnp.full_like(u, terms[-1])
    for term in terms[-2::-1]:
        total = total * u + term
    return total


def turns_cos_sin(turns):
    part = turns - jnp.round(turns)
    square = part * part
    half_sin = part * horner(SIN_TERMS, square)
    half_cos = horner(COS_TERMS, square)
    doubled = half_sin + half_sin
    return 1.0 - doubled * half_sin, doubled * half_cos


def angles_kernel(
    period, numbers_ref, blocks_ref, off_ref, tab_ref, slow_ref, uc_ref, us_ref, ac_ref, as_ref, bc_ref, bs_ref, delay_ref
):
    cells, tile = delay_ref.shape
    rows = lax.broadcasted_iota(jnp.int32, (tab_ref.shape[1], tile), 0)
    picks = jnp.where(rows == blocks_ref[...], 1.0, 0.0).astype(jnp.bfloat16)
    delay_ref[...] = jnp.dot(tab_ref[...], picks, preferred_element_type=jnp.float32)
    scale = 1.0 / period
    strip = 16
    lanes = 256

    def fill(index, _):
        row = pl.ds(pl.multiple_of(index // (tile // lanes) * strip, strip), strip)
        col = pl.ds(pl.multiple_of(index % (tile // lanes) * lanes, lanes), lanes)
        slow = slow_ref[row, :]
        geometry = off_ref[0:1, col] * slow[:, 0:1] + off_ref[1:2, col] * slow[:, 1:2]
        delay = delay_ref[row, col]
        uc_ref[row, col], us_ref[row, col] = turns_cos_sin((delay + geometry) * scale)
        for c, (cos_out, sin_out) in enumerate(((ac_ref, as_ref), (bc_ref, bs_ref))):
            number = numbers_ref[c].astype(jnp.float32)
            turns = number * delay * scale
            turns = (turns - jnp.round(turns)) + number * geometry * scale
            cos_out[row, col], sin_out[row, col] = turns_cos_sin(turns)
        return 0

    lax.fori_loop(0, cells // strip * (tile // lanes), fill, 0, unroll=2)


def angles(numbers, blocks, offsets, tab, slow, period):
    cells = tab.shape[0]
    stations = blocks.shape[1]
    tile = 512
    whole = lambda shape: pl.BlockSpec(shape, lambda i: (0,) * len(shape))
    return pl.pallas_call(
        functools.partial(angles_kernel, period),
        grid=(stations // tile,),
        out_shape=[jax.ShapeDtypeStruct((cells, stations), jnp.float32)] * 6,
        in_specs=[
            pl.BlockSpec(memory_space=pltpu.SMEM),
            pl.BlockSpec((1, tile), lambda i: (0, i)),
            pl.BlockSpec((2, tile), lambda i: (0, i)),
            whole(tab.shape),
            whole(slow.shape),
        ],
        out_specs=[pl.BlockSpec((cells, tile), lambda i: (0, i))] * 6,
        scratch_shapes=[pltpu.VMEM((cells, tile), jnp.float32)],
        compiler_params=pltpu.CompilerParams(vmem_limit_bytes=52 * 2**20),
        cost_estimate=pl.CostEstimate(flops=25 * 10**9, bytes_accessed=24 * cells * stations, transcendentals=0),
    )(numbers, blocks, offsets, tab, slow)


def bins_kernel(
    normalizer, place_ref, uc_ref, us_ref, fc_ref, fs_ref, x_ref, o0, o1, o2, o3, g_ref,
    cos_ref, sin_ref, pred_ref, res_ref
):
    bins, cells, tile = cos_ref.shape
    spot = place_ref[0]
    windows = x_ref.shape[1] // 2
    piece = o0.shape[2]
    step = pl.program_id(0)

    @pl.when(step == 0)
    def _():
        g_ref[...] = jnp.zeros_like(g_ref)

    strip = 16
    lanes = 256

    def fill(index, _):
        row = pl.ds(pl.multiple_of(index // (tile // lanes) * strip, strip), strip)
        col = pl.ds(pl.multiple_of(index % (tile // lanes) * lanes, lanes), lanes)
        unit_cos, unit_sin = uc_ref[row, col], us_ref[row, col]
        cos_old, sin_old = fc_ref[row, col], fs_ref[row, col]
        cos_ref[0, row, col] = cos_old.astype(jnp.bfloat16)
        sin_ref[0, row, col] = sin_old.astype(jnp.bfloat16)
        cos_now = cos_old * unit_cos - sin_old * unit_sin
        sin_now = sin_old * unit_cos + cos_old * unit_sin
        twice = unit_cos + unit_cos
        for b in range(1, bins):
            cos_ref[b, row, col] = cos_now.astype(jnp.bfloat16)
            sin_ref[b, row, col] = sin_now.astype(jnp.bfloat16)
            if b < bins - 1:
                cos_now, cos_old = twice * cos_now - cos_old, cos_now
                sin_now, sin_old = twice * sin_now - sin_old, sin_now
        return 0

    lax.fori_loop(0, cells // strip * (tile // lanes), fill, 0, unroll=2)

    across = (((1,), (1,)), ((), ()))

    for b in range(bins):
        stacked = x_ref[b]
        with_cos = jnp.dot(stacked, cos_ref[b], preferred_element_type=jnp.float32)
        with_sin = jnp.dot(stacked, sin_ref[b], preferred_element_type=jnp.float32)
        pred_ref[b, 0:windows] = (with_cos[:windows] + with_sin[windows:]) * normalizer
        pred_ref[b, windows:] = (with_cos[windows:] - with_sin[:windows]) * normalizer
        for d, o_ref in enumerate((o0, o1, o2, o3)):
            first = jnp.bitwise_xor(spot, d) * piece
            for k in range(2):
                at = pl.ds(pl.multiple_of(first + k * windows, piece), piece)
                res_ref[b, at, :] = (pred_ref[b, at, :] - o_ref[b, k].astype(jnp.float32)).astype(jnp.bfloat16)
        residual = res_ref[b]
        back_cos = lax.dot_general(residual, cos_ref[b], across, preferred_element_type=jnp.float32)
        back_sin = lax.dot_general(residual, sin_ref[b], across, preferred_element_type=jnp.float32)
        g_ref[b, 0:windows] += back_cos[:windows] - back_sin[windows:]
        g_ref[b, windows:] += back_cos[windows:] + back_sin[:windows]


def bins_gradient(place, unit, first, iterate, observed, normalizer):
    bins, rows, cells = iterate.shape
    stations = unit[0].shape[1]
    piece = observed[0].shape[2]
    tile = 512
    vm = pltpu.VMEM
    whole = lambda shape: pl.BlockSpec(shape, lambda i: (0,) * len(shape))
    return pl.pallas_call(
        functools.partial(bins_kernel, normalizer),
        grid=(stations // tile,),
        out_shape=jax.ShapeDtypeStruct((bins, rows, cells), jnp.float32),
        in_specs=[
            pl.BlockSpec(memory_space=pltpu.SMEM),
        ]
        + [pl.BlockSpec((cells, tile), lambda i: (0, i))] * 4
        + [whole(iterate.shape)]
        + [pl.BlockSpec((bins, 2, piece, tile), lambda i: (0, 0, 0, i))] * 4,
        out_specs=whole((bins, rows, cells)),
        scratch_shapes=[
            vm((bins, cells, tile), jnp.bfloat16),
            vm((bins, cells, tile), jnp.bfloat16),
            vm((bins, rows, tile), jnp.float32),
            vm((bins, rows, tile), jnp.bfloat16),
        ],
        compiler_params=pltpu.CompilerParams(vmem_limit_bytes=52 * 2**20),
        cost_estimate=pl.CostEstimate(
            flops=8 * bins * rows * cells * stations, bytes_accessed=16 * 2**20, transcendentals=0
        ),
    )(place, *unit, *first, iterate, *observed)


def local_grouped(freq_size, sta_size, spectra, current, previous, table, station_block, offsets, slowness, weights, momentum):
    period = 4 * F
    normalizer = 1.0 / math.sqrt(CELLS)
    bins = current.shape[0]
    cell_share = current.shape[3]
    half_windows = current.shape[2] // 2
    stations_here = station_block.shape[0]
    station_total = stations_here * sta_size
    me = lax.axis_index("freq")
    mine = lax.axis_index("sta")
    half, spot = me // 4, me % 4
    gradient_back = []
    rounded = current.astype(jnp.bfloat16)
    tab = jnp.bitwise_and(table, period - 1).astype(jnp.bfloat16).T
    slow = slowness.T
    blocks = station_block.reshape(1, -1)
    picks = []
    iterates = []
    for c in range(2):
        give = lax.rem(me + c, 2)
        sent = lax.dynamic_slice_in_dim(rounded, give * half_windows, half_windows, 2)
        perm = [(f, ((f + c) % 2) * 4 + f // 2) for f in range(freq_size)]
        got = lax.ppermute(sent, "freq", perm)
        iterates.append(got)
        gradient_back.append([(b, a) for a, b in perm])
    observed = []
    for c in range(2):
        odd = lax.rem(half + c, 2)
        parts = []
        for d in range(4):
            first = (2 * jnp.bitwise_xor(spot, d) + odd) * bins
            part = lax.dynamic_slice_in_dim(spectra, first, bins, 2).astype(jnp.bfloat16)
            parts.append(jnp.transpose(part, (2, 0, 1, 3)))
        if c == 0:
            parts, iterates = lax.optimization_barrier((parts, iterates))
            iterates = lax.all_gather(jnp.stack(iterates), "sta", axis=4, tiled=True)
        for d in range(1, 4):
            parts[d] = lax.ppermute(parts[d], "freq", [(f, f ^ d) for f in range(freq_size)])
        observed.append(parts)
    halves = []
    numbers = jnp.stack([(2 * spot + lax.rem(half + c, 2)) * bins + 1 for c in range(2)]).astype(jnp.int32)
    trig = angles(numbers, blocks, offsets, tab, slow, period)
    place = spot.reshape(1).astype(jnp.int32)
    for c in range(2):
        iterate = iterates[c].reshape(bins, 2 * half_windows, cell_share * sta_size)
        partial = bins_gradient(
            place, trig[0:2], trig[2 * c + 2 : 2 * c + 4], iterate, observed[c], normalizer
        )
        total = lax.dynamic_slice_in_dim(partial, mine * cell_share, cell_share, 2)
        for d in range(1, sta_size):
            sent = lax.dynamic_slice_in_dim(
                partial, jnp.bitwise_xor(mine, d) * cell_share, cell_share, 2
            )
            total = total + lax.ppermute(sent, "sta", [(s, s ^ d) for s in range(sta_size)])
        home = lax.ppermute(total * normalizer, "freq", gradient_back[c])
        halves.append(home.reshape(bins, 2, half_windows, cell_share))
    even = lax.rem(me, 2) == 0
    gradient = jnp.concatenate(
        [jnp.where(even, halves[0], halves[1]), jnp.where(even, halves[1], halves[0])], axis=2
    )
    step_size = CELLS / (math.sqrt(station_total) + math.sqrt(CELLS)) ** 2
    stepped = current - step_size * gradient
    threshold = step_size * weights
    squares = jnp.sum(stepped * stepped, axis=(0, 1))
    for d in (1, 2, 4):
        squares = squares + lax.ppermute(squares, "freq", [(f, f ^ d) for f in range(freq_size)])
    group_norm = jnp.sqrt(squares + 1e-06)
    estimate = stepped * jnp.maximum(0.0, 1.0 - threshold[None, :] / group_norm)
    momentum_now = momentum[0]
    momentum_next = (1.0 + jnp.sqrt(1.0 + 4.0 * momentum_now * momentum_now)) / 2.0
    extrapolated = estimate + (momentum_now - 1.0) / momentum_next * (estimate - previous)
    return (estimate, extrapolated)


def solution(mesh):
    freq_size, sta_size = mesh.shape["freq"], mesh.shape["sta"]
    body = local
    if freq_size == 8 and sta_size == 4:
        body = functools.partial(local_grouped, freq_size, sta_size)
    in_specs = (
        P(None, "freq", None, "sta"),
        P("freq", None, None, "sta"),
        P("freq", None, None, "sta"),
        P(),
        P("sta"),
        P(None, "sta"),
        P(),
        P("sta"),
        P(),
    )
    out_specs = (P("freq", None, None, "sta"), P("freq", None, None, "sta"))
    return jax.shard_map(body, mesh=mesh, in_specs=in_specs, out_specs=out_specs, check_vma=False)
```

```python
import functools
import math

import jax
import jax.numpy as jnp
from jax import lax
from jax.experimental import pallas as pl
from jax.experimental.pallas import tpu as pltpu
from jax.sharding import PartitionSpec as P

F = 64
CELLS = 512


def cell_block(cell_count):
    block_len = cell_count
    while block_len > 512 and block_len % 2 == 0:
        block_len = block_len // 2
    return block_len


def phases(number, delay_rows, off_rows, slow_cols, period):
    wrapped = number * delay_rows % period
    geometry = (
        off_rows[0][:, None] * slow_cols[0][None, :] + off_rows[1][:, None] * slow_cols[1][None, :]
    )
    phase_angle = (wrapped.astype(jnp.float32) + number.astype(jnp.float32) * geometry) * (
        2.0 * math.pi / period
    )
    return (jnp.cos(phase_angle).astype(jnp.bfloat16), jnp.sin(phase_angle).astype(jnp.bfloat16))


def forward_terms(cos_part, sin_part, iterate):
    window_count = iterate.shape[1]
    stacked = iterate.reshape(2 * window_count, iterate.shape[2])
    contract = (((1,), (1,)), ((), ()))
    with_cos = lax.dot_general(stacked, cos_part, contract, preferred_element_type=jnp.float32)
    with_sin = lax.dot_general(stacked, sin_part, contract, preferred_element_type=jnp.float32)
    real_part = with_cos[:window_count] + with_sin[window_count:]
    imag_part = with_cos[window_count:] - with_sin[:window_count]
    return jnp.stack([real_part, imag_part])


def adjoint_terms(cos_part, sin_part, residual):
    window_count = residual.shape[1]
    stacked = residual.reshape(2 * window_count, residual.shape[2])
    with_cos = jnp.dot(stacked, cos_part, preferred_element_type=jnp.float32)
    with_sin = jnp.dot(stacked, sin_part, preferred_element_type=jnp.float32)
    real_part = with_cos[:window_count] - with_sin[window_count:]
    imag_part = with_cos[window_count:] + with_sin[:window_count]
    return jnp.stack([real_part, imag_part])


def local(spectra, current, previous, table, station_block, offsets, slowness, weights, momentum):
    period = 4 * F
    normalizer = 1.0 / math.sqrt(CELLS)
    bin_count = current.shape[0]
    cell_share = current.shape[3]
    stations_here = station_block.shape[0]
    station_total = stations_here * lax.axis_size("sta")
    first_bin = lax.axis_index("freq") * bin_count
    relaid = lax.all_to_all(
        spectra.astype(jnp.bfloat16), "freq", split_axis=2, concat_axis=1, tiled=True
    ).astype(spectra.dtype)
    iterate_b = current.astype(jnp.bfloat16)
    segment = lax.all_gather(iterate_b, "sta", axis=3, tiled=True)
    cell_count = segment.shape[3]
    block_len = cell_block(cell_count)
    delay_rows = jnp.take(table, station_block, axis=0)
    bin_terms = []
    cos_blocks = []
    sin_blocks = []
    for add_bin_index in range(bin_count):
        cos_part, sin_part = phases(
            first_bin + add_bin_index + 1, delay_rows, offsets, slowness, period
        )
        cos_blocks.append(cos_part)
        sin_blocks.append(sin_part)
        bin_terms.append(
            forward_terms(cos_part, sin_part, segment[add_bin_index, :, :, 0:block_len])
        )
    running = jnp.stack(bin_terms)
    cos_all = jnp.stack(cos_blocks)
    sin_all = jnp.stack(sin_blocks)
    predicted, cos_all, sin_all = (running, cos_all, sin_all)
    bin_sums = []
    for bin_index in range(bin_count):
        residual = (predicted[bin_index] * normalizer - relaid[:, :, bin_index, :]).astype(
            jnp.bfloat16
        )
        bin_sums.append(
            adjoint_terms(cos_all[bin_index], sin_all[bin_index], residual) * normalizer
        )
    partial_sums = jnp.stack(bin_sums)
    summed = lax.psum(partial_sums, "sta")
    gradient = lax.dynamic_slice_in_dim(summed, lax.axis_index("sta") * cell_share, cell_share, 3)
    step_size = CELLS / (math.sqrt(station_total) + math.sqrt(CELLS)) ** 2
    stepped = current - step_size * gradient
    threshold = step_size * weights
    squares = jnp.sum(stepped * stepped, axis=(0, 1))
    group_norm = jnp.sqrt(lax.psum(squares, "freq") + 1e-06)
    estimate = stepped * jnp.maximum(0.0, 1.0 - threshold[None, :] / group_norm)
    momentum_now = momentum[0]
    momentum_next = (1.0 + jnp.sqrt(1.0 + 4.0 * momentum_now * momentum_now)) / 2.0
    extrapolated = estimate + (momentum_now - 1.0) / momentum_next * (estimate - previous)
    return (estimate, extrapolated)


SIN_TERMS = (3.1415926535362892, -5.167712764624382, 2.5501633189428987, -0.5992521977810126, 0.08205040162239277, -0.007028386120383206)
COS_TERMS = (0.9999999997799041, -4.934802137078749, 4.058709159554242, -1.335212003029471, 0.23493731372678894, -0.024396324214549327)


def horner(terms, u):
    total = jnp.full_like(u, terms[-1])
    for term in terms[-2::-1]:
        total = total * u + term
    return total


def turns_cos_sin(turns):
    part = turns - jnp.round(turns)
    square = part * part
    half_sin = part * horner(SIN_TERMS, square)
    half_cos = horner(COS_TERMS, square)
    doubled = half_sin + half_sin
    return 1.0 - doubled * half_sin, doubled * half_cos


def angles_kernel(
    period, numbers_ref, blocks_ref, off_ref, tab_ref, slow_ref, uc_ref, us_ref, ac_ref, as_ref, bc_ref, bs_ref, delay_ref
):
    cells, tile = delay_ref.shape
    rows = lax.broadcasted_iota(jnp.int32, (tab_ref.shape[1], tile), 0)
    picks = jnp.where(rows == blocks_ref[...], 1.0, 0.0).astype(jnp.bfloat16)
    delay_ref[...] = jnp.dot(tab_ref[...], picks, preferred_element_type=jnp.float32)
    scale = 1.0 / period
    strip = 16
    lanes = 256

    def fill(index, _):
        row = pl.ds(pl.multiple_of(index // (tile // lanes) * strip, strip), strip)
        col = pl.ds(pl.multiple_of(index % (tile // lanes) * lanes, lanes), lanes)
        slow = slow_ref[row, :]
        geometry = off_ref[0:1, col] * slow[:, 0:1] + off_ref[1:2, col] * slow[:, 1:2]
        delay = delay_ref[row, col]
        uc_ref[row, col], us_ref[row, col] = turns_cos_sin((delay + geometry) * scale)
        for c, (cos_out, sin_out) in enumerate(((ac_ref, as_ref), (bc_ref, bs_ref))):
            number = numbers_ref[c].astype(jnp.float32)
            turns = number * delay * scale
            turns = (turns - jnp.round(turns)) + number * geometry * scale
            cos_out[row, col], sin_out[row, col] = turns_cos_sin(turns)
        return 0

    lax.fori_loop(0, cells // strip * (tile // lanes), fill, 0, unroll=2)


def angles(numbers, blocks, offsets, tab, slow, period):
    cells = tab.shape[0]
    stations = blocks.shape[1]
    tile = 512
    whole = lambda shape: pl.BlockSpec(shape, lambda i: (0,) * len(shape))
    return pl.pallas_call(
        functools.partial(angles_kernel, period),
        grid=(stations // tile,),
        out_shape=[jax.ShapeDtypeStruct((cells, stations), jnp.float32)] * 6,
        in_specs=[
            pl.BlockSpec(memory_space=pltpu.SMEM),
            pl.BlockSpec((1, tile), lambda i: (0, i)),
            pl.BlockSpec((2, tile), lambda i: (0, i)),
            whole(tab.shape),
            whole(slow.shape),
        ],
        out_specs=[pl.BlockSpec((cells, tile), lambda i: (0, i))] * 6,
        scratch_shapes=[pltpu.VMEM((cells, tile), jnp.float32)],
        compiler_params=pltpu.CompilerParams(vmem_limit_bytes=52 * 2**20),
        cost_estimate=pl.CostEstimate(flops=25 * 10**9, bytes_accessed=24 * cells * stations, transcendentals=0),
    )(numbers, blocks, offsets, tab, slow)


def bins_kernel(
    normalizer, place_ref, uc_ref, us_ref, fc_ref, fs_ref, x_ref, o0, o1, o2, o3, g_ref,
    cos_ref, sin_ref, pred_ref, res_ref
):
    bins, cells, tile = cos_ref.shape
    spot = place_ref[0]
    windows = x_ref.shape[1] // 2
    piece = o0.shape[2]
    step = pl.program_id(0)

    @pl.when(step == 0)
    def _():
        g_ref[...] = jnp.zeros_like(g_ref)

    strip = 16
    lanes = 256

    def fill(index, _):
        row = pl.ds(pl.multiple_of(index // (tile // lanes) * strip, strip), strip)
        col = pl.ds(pl.multiple_of(index % (tile // lanes) * lanes, lanes), lanes)
        unit_cos, unit_sin = uc_ref[row, col], us_ref[row, col]
        cos_old, sin_old = fc_ref[row, col], fs_ref[row, col]
        cos_ref[0, row, col] = cos_old.astype(jnp.bfloat16)
        sin_ref[0, row, col] = sin_old.astype(jnp.bfloat16)
        cos_now = cos_old * unit_cos - sin_old * unit_sin
        sin_now = sin_old * unit_cos + cos_old * unit_sin
        twice = unit_cos + unit_cos
        for b in range(1, bins):
            cos_ref[b, row, col] = cos_now.astype(jnp.bfloat16)
            sin_ref[b, row, col] = sin_now.astype(jnp.bfloat16)
            if b < bins - 1:
                cos_now, cos_old = twice * cos_now - cos_old, cos_now
                sin_now, sin_old = twice * sin_now - sin_old, sin_now
        return 0

    lax.fori_loop(0, cells // strip * (tile // lanes), fill, 0, unroll=2)

    across = (((1,), (1,)), ((), ()))

    for b in range(bins):
        stacked = x_ref[b]
        with_cos = jnp.dot(stacked, cos_ref[b], preferred_element_type=jnp.float32)
        with_sin = jnp.dot(stacked, sin_ref[b], preferred_element_type=jnp.float32)
        pred_ref[b, 0:windows] = (with_cos[:windows] + with_sin[windows:]) * normalizer
        pred_ref[b, windows:] = (with_cos[windows:] - with_sin[:windows]) * normalizer
        for d, o_ref in enumerate((o0, o1, o2, o3)):
            first = jnp.bitwise_xor(spot, d) * piece
            for k in range(2):
                at = pl.ds(pl.multiple_of(first + k * windows, piece), piece)
                res_ref[b, at, :] = (pred_ref[b, at, :] - o_ref[b, k].astype(jnp.float32)).astype(jnp.bfloat16)
        residual = res_ref[b]
        back_cos = lax.dot_general(residual, cos_ref[b], across, preferred_element_type=jnp.float32)
        back_sin = lax.dot_general(residual, sin_ref[b], across, preferred_element_type=jnp.float32)
        g_ref[b, 0:windows] += back_cos[:windows] - back_sin[windows:]
        g_ref[b, windows:] += back_cos[windows:] + back_sin[:windows]


def bins_gradient(place, unit, first, iterate, observed, normalizer):
    bins, rows, cells = iterate.shape
    stations = unit[0].shape[1]
    piece = observed[0].shape[2]
    tile = 512
    vm = pltpu.VMEM
    whole = lambda shape: pl.BlockSpec(shape, lambda i: (0,) * len(shape))
    return pl.pallas_call(
        functools.partial(bins_kernel, normalizer),
        grid=(stations // tile,),
        out_shape=jax.ShapeDtypeStruct((bins, rows, cells), jnp.float32),
        in_specs=[
            pl.BlockSpec(memory_space=pltpu.SMEM),
        ]
        + [pl.BlockSpec((cells, tile), lambda i: (0, i))] * 4
        + [whole(iterate.shape)]
        + [pl.BlockSpec((bins, 2, piece, tile), lambda i: (0, 0, 0, i))] * 4,
        out_specs=whole((bins, rows, cells)),
        scratch_shapes=[
            vm((bins, cells, tile), jnp.bfloat16),
            vm((bins, cells, tile), jnp.bfloat16),
            vm((bins, rows, tile), jnp.float32),
            vm((bins, rows, tile), jnp.bfloat16),
        ],
        compiler_params=pltpu.CompilerParams(vmem_limit_bytes=52 * 2**20),
        cost_estimate=pl.CostEstimate(
            flops=8 * bins * rows * cells * stations, bytes_accessed=16 * 2**20, transcendentals=0
        ),
    )(place, *unit, *first, iterate, *observed)


def local_grouped(freq_size, sta_size, spectra, current, previous, table, station_block, offsets, slowness, weights, momentum):
    period = 4 * F
    normalizer = 1.0 / math.sqrt(CELLS)
    bins = current.shape[0]
    cell_share = current.shape[3]
    half_windows = current.shape[2] // 2
    stations_here = station_block.shape[0]
    station_total = stations_here * sta_size
    me = lax.axis_index("freq")
    mine = lax.axis_index("sta")
    half, spot = me // 4, me % 4
    gradient_back = []
    rounded = current.astype(jnp.bfloat16)
    tab = jnp.bitwise_and(table, period - 1).astype(jnp.bfloat16).T
    slow = slowness.T
    blocks = station_block.reshape(1, -1)
    picks = []
    iterates = []
    for c in range(2):
        give = lax.rem(me + c, 2)
        sent = lax.dynamic_slice_in_dim(rounded, give * half_windows, half_windows, 2)
        perm = [(f, ((f + c) % 2) * 4 + f // 2) for f in range(freq_size)]
        got = lax.ppermute(sent, "freq", perm)
        iterates.append(got)
        gradient_back.append([(b, a) for a, b in perm])
    observed = []
    for c in range(2):
        odd = lax.rem(half + c, 2)
        parts = []
        for d in range(4):
            first = (2 * jnp.bitwise_xor(spot, d) + odd) * bins
            part = lax.dynamic_slice_in_dim(spectra, first, bins, 2).astype(jnp.bfloat16)
            parts.append(jnp.transpose(part, (2, 0, 1, 3)))
        if c == 0:
            parts, iterates = lax.optimization_barrier((parts, iterates))
            iterates = lax.all_gather(jnp.stack(iterates), "sta", axis=4, tiled=True)
        for d in range(1, 4):
            parts[d] = lax.ppermute(parts[d], "freq", [(f, f ^ d) for f in range(freq_size)])
        observed.append(parts)
    halves = []
    numbers = jnp.stack([(2 * spot + lax.rem(half + c, 2)) * bins + 1 for c in range(2)]).astype(jnp.int32)
    trig = angles(numbers, blocks, offsets, tab, slow, period)
    place = spot.reshape(1).astype(jnp.int32)
    for c in range(2):
        iterate = iterates[c].reshape(bins, 2 * half_windows, cell_share * sta_size)
        partial = bins_gradient(
            place, trig[0:2], trig[2 * c + 2 : 2 * c + 4], iterate, observed[c], normalizer
        )
        share = lambda d: lax.dynamic_slice_in_dim(
            partial, jnp.bitwise_xor(mine, d) * cell_share, cell_share, 2
        )
        swap = lambda block, d: lax.ppermute(block, "sta", [(s, s ^ d) for s in range(sta_size)])
        across = share(2) + swap(share(3), 1)
        total = share(0) + swap(share(1), 1) + swap(across, 2)
        home = lax.ppermute(total * normalizer, "freq", gradient_back[c])
        halves.append(home.reshape(bins, 2, half_windows, cell_share))
    even = lax.rem(me, 2) == 0
    gradient = jnp.concatenate(
        [jnp.where(even, halves[0], halves[1]), jnp.where(even, halves[1], halves[0])], axis=2
    )
    step_size = CELLS / (math.sqrt(station_total) + math.sqrt(CELLS)) ** 2
    stepped = current - step_size * gradient
    threshold = step_size * weights
    squares = jnp.sum(stepped * stepped, axis=(0, 1))
    for d in (1, 2, 4):
        squares = squares + lax.ppermute(squares, "freq", [(f, f ^ d) for f in range(freq_size)])
    group_norm = jnp.sqrt(squares + 1e-06)
    estimate = stepped * jnp.maximum(0.0, 1.0 - threshold[None, :] / group_norm)
    momentum_now = momentum[0]
    momentum_next = (1.0 + jnp.sqrt(1.0 + 4.0 * momentum_now * momentum_now)) / 2.0
    extrapolated = estimate + (momentum_now - 1.0) / momentum_next * (estimate - previous)
    return (estimate, extrapolated)


def solution(mesh):
    freq_size, sta_size = mesh.shape["freq"], mesh.shape["sta"]
    body = local
    if freq_size == 8 and sta_size == 4:
        body = functools.partial(local_grouped, freq_size, sta_size)
    in_specs = (
        P(None, "freq", None, "sta"),
        P("freq", None, None, "sta"),
        P("freq", None, None, "sta"),
        P(),
        P("sta"),
        P(None, "sta"),
        P(),
        P("sta"),
        P(),
    )
    out_specs = (P("freq", None, None, "sta"), P("freq", None, None, "sta"))
    return jax.shard_map(body, mesh=mesh, in_specs=in_specs, out_specs=out_specs, check_vma=False)
```
